128 devices in a mesh: run: 16 (over x_hi, z, core), mz: 8 (over x_lo, y).
Axes of the slice: x: 4 (x_hi: 2, x_lo: 2; x = x_hi * 2 + x_lo), y: 4, z: 4, core: 2. Of those that a mesh axis runs over, the one named last changes fastest.
Arguments:
- lcms: bfloat16 [1024, 256, 4096], P('run', None, 'mz'), may hold values from -600 to 600
- spectra: float32 [1024, 65536], P('run', 'mz'), may hold values from -200 to 200
- scan_factor: float32 [64, 256], replicated, may hold values from 0.05 to 0.9
- mz_factor: float32 [64, 4096], P(None, 'mz'), may hold values from 0 to 1.7
- ppm_factor: float32 [64, 65536], P(None, 'mz'), may hold values from 0 to 1.7
Outputs:
- sample_factor: float32 [1024, 64], P('run')
- ppm_new: float32 [64, 65536], P(None, ('mz', 'run'))
The draws below stay inside these ranges and needn't reach their ends.
All inputs are finite; a program needn't handle non-finite values.
Results may differ from the reference program's by a relative error of at most 0.0048.
Values sent between devices are 32-bit elements; how exact they have to be, the bound alone decides.
A program may use at most 64 MiB of HBM per device.

```python
import jax
import jax.numpy as jnp
from jax import lax

RUN_DEV = 64
SCANS = 256
MZ = 4096
PPM = 65536
RANK = 64
RUNS = 1024


def ramped_factor(key, columns):
    first_key = jax.random.fold_in(key, 0)
    ramp = 0.6 + 1.2 * jnp.arange(columns, dtype=jnp.float32) / (columns - 1)
    values = jax.random.uniform(first_key, (RANK, columns), jnp.float32, 0.05, 0.9)
    return values * ramp[None, :]


def draw_mz_factor(key, part):
    return ramped_factor(jax.random.fold_in(key, 11), MZ)


def draw_ppm_factor(key, part):
    return ramped_factor(jax.random.fold_in(key, 23), PPM)


def shard_levels(rng, shape, cuts, least, largest):
    level, own = 1.0, jax.random.fold_in(rng, 6)
    for dim, blocks in cuts:
        heights = jnp.exp(jax.random.uniform(jax.random.fold_in(own, dim), (blocks,), jnp.float32, least / len(cuts), largest / len(cuts)))
        level = level * jnp.repeat(heights, shape[dim] // blocks).reshape([-1 if axis == dim else 1 for axis in range(len(shape))])
    return level


def centred(own_key, shape, deviation, bound, shards=(), kind=jnp.bfloat16):
    values = jax.random.normal(own_key, shape, jnp.float32) * deviation
    if len(shards) > 0:
        values = shard_levels(own_key, shape, shards, -0.22, 0.18) * values
    return jnp.clip(values, min=-bound, max=bound).astype(kind)


def setup_inputs(seed: int = 0) -> dict:
    arg_keys = jax.random.split(jax.random.key(seed), 6)
    lcms = centred(arg_keys[0], (RUNS, SCANS, MZ), 100.0, 600.0, ((0, 16), (2, 8)))
    spectra = centred(arg_keys[1], (RUNS, PPM), 32.0, 200.0, ((0, 16), (1, 8)), jnp.float32)
    scan_factor = jnp.clip(jax.random.uniform(arg_keys[2], (RANK, SCANS), jnp.float32, 0.05, 0.9), 0.05, 0.9)
    mz_factor = draw_mz_factor(jax.random.fold_in(arg_keys[5], 71), 0)
    ppm_factor = draw_ppm_factor(jax.random.fold_in(arg_keys[5], 71), 0)
    return {"lcms": lcms, "spectra": spectra, "scan_factor": scan_factor, "mz_factor": mz_factor, "ppm_factor": ppm_factor}


def solve_rows(gram_matrix, right_rows):
    lower_factor = jnp.linalg.cholesky(gram_matrix)
    return jax.scipy.linalg.cho_solve((lower_factor, True), right_rows.T).T

def reference(lcms, spectra, scan_factor, mz_factor, ppm_factor):
    highest = lax.Precision.HIGHEST
    scan_bf = scan_factor.astype(jnp.bfloat16).astype(jnp.float32)
    blocks = lcms.reshape(RUNS // RUN_DEV, RUN_DEV, SCANS, MZ)

    def one_block(run_block):
        tensor = jnp.einsum('ijk,rj->irk', run_block.astype(jnp.float32), scan_bf, precision=highest)
        return jnp.sum(tensor * mz_factor[None], axis=2)
    lcms_part = lax.map(one_block, blocks).reshape(RUNS, RANK)
    scan_gram = jnp.dot(scan_factor, scan_factor.T, precision=highest)
    mz_gram = jnp.dot(mz_factor, mz_factor.T, precision=highest)
    ppm_gram = jnp.dot(ppm_factor, ppm_factor.T, precision=highest)
    lcms_gram = scan_gram * mz_gram
    nmr_part = lax.dot_general(spectra, ppm_factor, (((1,), (1,)), ((), ())), precision=highest)
    sample_first = solve_rows(lcms_gram + ppm_gram, lcms_part + nmr_part)
    sample_gram = jnp.dot(sample_first.T, sample_first, precision=highest)
    projected = jnp.dot(sample_first.T, spectra, precision=highest)
    ppm_new = jax.scipy.linalg.cho_solve((jnp.linalg.cholesky(sample_gram), True), projected)
    nmr_fit = lax.dot_general(spectra, ppm_new, (((1,), (1,)), ((), ())), precision=highest)
    new_gram = jnp.dot(ppm_new, ppm_new.T, precision=highest)
    sample_factor = solve_rows(lcms_gram + new_gram, lcms_part + nmr_fit)
    return (sample_factor, ppm_new)
```

```python
import functools

import jax
import jax.numpy as jnp
from jax import lax
from jax.experimental import pallas as pl
from jax.experimental.pallas import tpu as pltpu
from jax.sharding import PartitionSpec as P

MESH = pl.DeviceIdType.MESH
HIGHEST = lax.Precision.HIGHEST
F32 = jnp.float32
BF16 = jnp.bfloat16
NT = (((1,), (1,)), ((), ()))
TN = (((0,), (0,)), ((), ()))
NN = (((1,), (0,)), ((), ()))

N_RUN = 16
N_MZ = 8
RANK = 64
RUNS = 64
SCANS = 256
CHANNELS = 512
POSITIONS = 8192
OWNED = 512
LCMS_PARTS = 16
FIRST_BATCH = (2, 14, 8, 1, 4, 10, 6)
SECOND_BATCH = (12, 3)
THIRD_BATCH = (15, 9, 5, 11, 7, 13)


def split(value):
    high = value.astype(BF16)
    low = (value - high.astype(F32)).astype(BF16)
    return high, low


def dot(left, right, dims, precision=None):
    return lax.dot_general(left, right, dims, precision=precision, preferred_element_type=F32)


def small_inverse(block):
    if len(block) == 2:
        scale = 1.0 / (block[0][0] * block[1][1] - block[0][1] * block[0][1])
        off = -block[0][1] * scale
        return [[block[1][1] * scale, off], [off, block[0][0] * scale]]
    half = range(2)
    upper = small_inverse([[block[i][j] for j in half] for i in half])
    cross = [[block[i][2 + j] for j in half] for i in half]
    mixed = [[upper[i][0] * cross[0][j] + upper[i][1] * cross[1][j] for j in half] for i in half]
    rest = [[None, None], [None, None]]
    for i in half:
        for j in range(i, 2):
            rest[i][j] = block[2 + i][2 + j] - (cross[0][i] * mixed[0][j] + cross[1][i] * mixed[1][j])
    rest[1][0] = rest[0][1]
    lower = small_inverse(rest)
    side = [[mixed[i][0] * lower[0][j] + mixed[i][1] * lower[1][j] for j in half] for i in half]
    result = [[None] * 4 for _ in range(4)]
    for i in half:
        for j in half:
            result[i][j] = upper[i][j] + (side[i][0] * mixed[j][0] + side[i][1] * mixed[j][1])
            result[i][2 + j] = -side[i][j]
            result[2 + j][i] = -side[i][j]
            result[2 + i][2 + j] = lower[i][j]
    return result


def spd_inverse(matrix):
    size, wide, pivot = RANK, 2 * RANK, 4
    tiles = []
    lane = lax.broadcasted_iota(jnp.int32, (8, wide), 1)
    sub = lax.broadcasted_iota(jnp.int32, (8, wide), 0)
    for t in range(size // 8):
        unit = (lane == sub + (size + 8 * t)).astype(F32)
        left = jnp.concatenate([matrix[8 * t : 8 * t + 8], jnp.zeros((8, size), F32)], axis=1)
        tiles.append(left + unit)
    for j in range(0, size, pivot):
        home, first = j // 8, j % 8
        rows = [jnp.broadcast_to(tiles[home][first + k : first + k + 1], (8, wide)) for k in range(pivot)]
        block = [[None] * pivot for _ in range(pivot)]
        for k in range(pivot):
            for m in range(k, pivot):
                block[k][m] = jnp.broadcast_to(rows[k][:, j + m : j + m + 1], (8, wide))
                block[m][k] = block[k][m]
        inverse = small_inverse(block)
        fresh = []
        for k in range(pivot):
            fresh.append((inverse[k][0] * rows[0] + inverse[k][1] * rows[1]) + (inverse[k][2] * rows[2] + inverse[k][3] * rows[3]))
        for t in range(size // 8):
            tile = tiles[t]
            taken = [jnp.broadcast_to(tile[:, j + k : j + k + 1], (8, wide)) * fresh[k] for k in range(pivot)]
            tile = tile - ((taken[0] + taken[1]) + (taken[2] + taken[3]))
            if t == home:
                for k in range(pivot):
                    tile = jnp.where(sub == first + k, fresh[k], tile)
            tiles[t] = tile
    return jnp.concatenate([tile[:, size:] for tile in tiles], axis=0)


def pack(value):
    return jnp.concatenate([value[0:32], value[32:64]], axis=1)


def unpack(value):
    return jnp.concatenate([value[:, 0:64], value[:, 64:128]], axis=0)


def twice(value):
    empty = jnp.zeros_like(value)
    return jnp.concatenate(
        [jnp.concatenate([value, empty], axis=1), jnp.concatenate([empty, value], axis=1)], axis=0
    )


def fold(value):
    wide = value[0:64] + value[64:128]
    return wide[:, 0:64] + wide[:, 64:128]


def kernel(
    lcms_hbm, spectra_hbm, scan_hbm, mz_hbm, ppm_hbm,
    sample_ref, new_ref,
    lcms_v, spectra_v, scan_v, mz_v, ppm_v, lcms_acc, columns_v,
    gram_in, right_in, right_all, fit_out, fit_in, new_gram_in, last_in, last_gram_in,
    own_sem, lcms_sem, all_send, all_recv,
    gram_send, gram_recv, right_send, right_recv, share_send, share_recv,
    fit_send, fit_recv, ng_send, ng_recv, last_send, last_recv, lg_send, lg_recv,
):
    run = lax.axis_index("run")
    mz = lax.axis_index("mz")

    def run_peer(k):
        return (lax.rem(run + k, N_RUN), mz)

    def mz_peer(k):
        return (run, lax.rem(mz + k, N_MZ))

    loads = [
        pltpu.make_async_copy(mz_hbm, mz_v, own_sem.at[0]),
        pltpu.make_async_copy(scan_hbm, scan_v, own_sem.at[1]),
        pltpu.make_async_copy(ppm_hbm, ppm_v, own_sem.at[2]),
        pltpu.make_async_copy(spectra_hbm, spectra_v, own_sem.at[3]),
    ]
    for load in loads:
        load.start()
    per_part = RUNS // LCMS_PARTS
    lcms_loads = [
        pltpu.make_async_copy(
            lcms_hbm.at[pl.ds(c * per_part, per_part)], lcms_v.at[pl.ds(c * per_part, per_part)], lcms_sem.at[c]
        )
        for c in range(LCMS_PARTS)
    ]
    for load in lcms_loads:
        load.start()

    barrier = pltpu.get_barrier_semaphore()
    for k in range(1, N_RUN):
        pl.semaphore_signal(barrier, inc=1, device_id=run_peer(k), device_id_type=MESH)
    for k in range(1, N_MZ):
        pl.semaphore_signal(barrier, inc=1, device_id=mz_peer(k), device_id_type=MESH)
    pl.semaphore_wait(barrier, N_RUN + N_MZ - 2)

    def place(ref):
        return ref.at[run // 4, :, pl.ds(pl.multiple_of(lax.rem(run, 4) * 32, 32), 32), :]

    def piece(owner):
        return spectra_hbm.at[:, :, pl.ds(pl.multiple_of(owner * OWNED, OWNED), OWNED)]

    own_piece = pltpu.make_async_copy(piece(run), place(columns_v), own_sem.at[4])
    own_piece.start()
    spread = {}
    for k in FIRST_BATCH + SECOND_BATCH + THIRD_BATCH:
        peer = run_peer(k)
        spread[k] = pltpu.make_async_remote_copy(
            src_ref=piece(peer[0]), dst_ref=place(columns_v),
            send_sem=all_send.at[k], recv_sem=all_recv.at[k], device_id=peer, device_id_type=MESH,
        )
    for k in FIRST_BATCH:
        spread[k].start()

    def exchange(peer_of, count, source_of, target, send, recv):
        copies = []
        for k in range(1, count):
            peer = peer_of(k)
            copies.append(pltpu.make_async_remote_copy(
                src_ref=source_of(peer), dst_ref=target,
                send_sem=send.at[k], recv_sem=recv.at[k], device_id=peer, device_id_type=MESH,
            ))
        for copy in copies:
            copy.start()
        return copies

    def arrive(copies):
        for copy in copies:
            copy.wait_recv()

    def total(ref, count):
        value = ref[0]
        for k in range(1, count):
            value = value + ref[k]
        return value

    for load in loads:
        load.wait()
    mz_high, mz_low = split(mz_v[...])
    mz_parts = jnp.concatenate([mz_high, mz_low], axis=0)
    mz_gram = fold(dot(mz_parts, mz_parts, NT))
    step = 1024
    sums = jnp.zeros((256, 128), F32)
    for c in range(POSITIONS // step):
        spec = jnp.concatenate([spectra_v[0, :, c * step : (c + 1) * step], spectra_v[1, :, c * step : (c + 1) * step]], axis=0)
        spec_high, spec_low = split(spec)
        ppm_high, ppm_low = split(ppm_v[:, c * step : (c + 1) * step])
        sums = sums + dot(
            jnp.concatenate([spec_high, spec_low, ppm_high, ppm_low], axis=0),
            jnp.concatenate([ppm_high, ppm_low], axis=0), NT,
        )
    nmr_local = fold(sums[0:128])
    ppm_gram = fold(sums[128:256])
    gram_in[mz] = jnp.concatenate([mz_gram, ppm_gram], axis=1)
    gram_copies = exchange(mz_peer, N_MZ, lambda peer: gram_in.at[mz], gram_in.at[mz], gram_send, gram_recv)

    scan = scan_v[...]
    scan_bf = scan.astype(BF16).astype(F32)
    scan_rows = jnp.concatenate([scan_bf, scan_bf], axis=0).T
    for c in range(LCMS_PARTS):
        lcms_loads[c].wait()
        found = []
        for i in range(per_part):
            inner = dot(lcms_v[c * per_part + i], mz_parts, NT)
            found.append(jnp.sum(inner * scan_rows, axis=0, keepdims=True))
        lcms_acc[pl.ds(c * per_part, per_part), :] = jnp.concatenate(found, axis=0)
    lcms_local = lcms_acc[:, 0:64] + lcms_acc[:, 64:128]
    lcms_packed = pack(lcms_local)
    right_in[mz] = pack(lcms_local + nmr_local)
    right_copies = exchange(mz_peer, N_MZ, lambda peer: right_in.at[mz], right_in.at[mz], right_send, right_recv)
    for k in SECOND_BATCH:
        spread[k].start()

    arrive(gram_copies)
    grams = total(gram_in, N_MZ)
    lcms_gram = dot(scan, scan, NT, HIGHEST) * grams[:, 0:64]
    first_inverse = twice(spd_inverse(lcms_gram + grams[:, 64:128]))

    arrive(right_copies)
    right_all[run] = total(right_in, N_MZ)
    share_copies = exchange(run_peer, N_RUN, lambda peer: right_all.at[run], right_all.at[run], share_send, share_recv)
    for k in THIRD_BATCH:
        spread[k].start()
    arrive(share_copies)
    first = dot(right_all[...].reshape(512, 128), first_inverse, NN, HIGHEST)
    products = dot(first, first, TN, HIGHEST)
    sample_gram = products[0:64, 0:64] + products[64:128, 64:128]
    weights = dot(first, twice(spd_inverse(sample_gram)), NN, HIGHEST).T

    own_piece.wait()
    arrive([spread[k] for k in spread])
    ppm_new = jnp.zeros((RANK, OWNED), F32)
    for g in range(4):
        rows = slice(128 * g, 128 * g + 128)
        part_high, part_low = split(jnp.concatenate([weights[0:64, rows], weights[64:128, rows]], axis=1))
        high, low = split(columns_v[g].reshape(256, OWNED))
        both = dot(jnp.concatenate([part_high, part_low], axis=0), high, NN)
        ppm_new = ppm_new + ((both[0:64] + both[64:128]) + dot(part_high, low, NN))
    new_ref[...] = ppm_new
    new_high, new_low = split(ppm_new)
    new_parts = jnp.concatenate([new_high, new_low], axis=0)
    new_gram_in[run] = pack(fold(dot(new_parts, new_parts, NT)))
    ng_copies = exchange(run_peer, N_RUN, lambda peer: new_gram_in.at[run], new_gram_in.at[run], ng_send, ng_recv)
    for g in range(4):
        high, low = split(columns_v[g].reshape(256, OWNED))
        both = dot(high, new_parts, NT) + dot(low, new_parts, NT)
        fit = both[:, 0:64] + both[:, 64:128]
        fit_out[pl.ds(4 * g, 4)] = jnp.concatenate([fit[0:128], fit[128:256]], axis=1).reshape(4, 32, 128)
    fit_in[run] = fit_out[run]
    fit_copies = exchange(run_peer, N_RUN, lambda peer: fit_out.at[peer[0]], fit_in.at[run], fit_send, fit_recv)

    arrive(ng_copies)
    last_gram_in[mz] = total(new_gram_in, N_RUN)
    lg_copies = exchange(mz_peer, N_MZ, lambda peer: last_gram_in.at[mz], last_gram_in.at[mz], lg_send, lg_recv)
    arrive(fit_copies)
    last_in[mz] = total(fit_in, N_RUN) + lcms_packed
    last_copies = exchange(mz_peer, N_MZ, lambda peer: last_in.at[mz], last_in.at[mz], last_send, last_recv)
    arrive(lg_copies)
    last_inverse = twice(spd_inverse(lcms_gram + unpack(total(last_gram_in, N_MZ))))
    arrive(last_copies)
    sample_ref[...] = unpack(dot(total(last_in, N_MZ), last_inverse, NN, HIGHEST))

    for copies in (gram_copies, right_copies, share_copies, ng_copies, fit_copies, lg_copies, last_copies):
        for copy in copies:
            copy.wait_send()
    for k in spread:
        spread[k].wait_send()


def per_device(lcms, spectra, scan_factor, mz_factor, ppm_factor):
    hbm = pl.BlockSpec(memory_space=pl.ANY)
    vmem = pl.BlockSpec(memory_space=pltpu.VMEM)
    sems = pltpu.SemaphoreType.DMA
    return pl.pallas_call(
        kernel,
        out_shape=(
            jax.ShapeDtypeStruct((RUNS, RANK), F32),
            jax.ShapeDtypeStruct((RANK, OWNED), F32),
        ),
        in_specs=[hbm] * 5,
        out_specs=(vmem, vmem),
        scratch_shapes=[
            pltpu.VMEM((RUNS, SCANS, CHANNELS), BF16),
            pltpu.VMEM((2, 32, POSITIONS), F32),
            pltpu.VMEM((RANK, SCANS), F32),
            pltpu.VMEM((RANK, CHANNELS), F32),
            pltpu.VMEM((RANK, POSITIONS), F32),
            pltpu.VMEM((RUNS, 128), F32),
            pltpu.VMEM((4, 2, 128, OWNED), F32),
            pltpu.VMEM((N_MZ, 64, 128), F32),
            pltpu.VMEM((N_MZ, 32, 128), F32),
            pltpu.VMEM((N_RUN, 32, 128), F32),
            pltpu.VMEM((N_RUN, 32, 128), F32),
            pltpu.VMEM((N_RUN, 32, 128), F32),
            pltpu.VMEM((N_RUN, 32, 128), F32),
            pltpu.VMEM((N_MZ, 32, 128), F32),
            pltpu.VMEM((N_MZ, 32, 128), F32),
            sems((5,)), sems((LCMS_PARTS,)), sems((N_RUN,)), sems((N_RUN,)),
            sems((N_MZ,)), sems((N_MZ,)), sems((N_MZ,)), sems((N_MZ,)), sems((N_RUN,)), sems((N_RUN,)),
            sems((N_RUN,)), sems((N_RUN,)), sems((N_RUN,)), sems((N_RUN,)),
            sems((N_MZ,)), sems((N_MZ,)), sems((N_MZ,)), sems((N_MZ,)),
        ],
        compiler_params=pltpu.CompilerParams(
            collective_id=0, has_side_effects=True, vmem_limit_bytes=50 * 2**20
        ),
    )(lcms, spectra.reshape(2, 32, POSITIONS), scan_factor, mz_factor, ppm_factor)


def solution(mesh):
    return jax.shard_map(
        per_device,
        mesh=mesh,
        in_specs=(P("run", None, "mz"), P("run", "mz"), P(), P(None, "mz"), P(None, "mz")),
        out_specs=(P("run", None), P(None, ("mz", "run"))),
        check_vma=False,
    )
```

```python
import functools

import jax
import jax.numpy as jnp
from jax import lax
from jax.experimental import pallas as pl
from jax.experimental.pallas import tpu as pltpu
from jax.sharding import PartitionSpec as P

MESH = pl.DeviceIdType.MESH
HIGHEST = lax.Precision.HIGHEST
F32 = jnp.float32
BF16 = jnp.bfloat16
NT = (((1,), (1,)), ((), ()))
TN = (((0,), (0,)), ((), ()))
NN = (((1,), (0,)), ((), ()))

N_RUN = 16
N_MZ = 8
RANK = 64
RUNS = 64
SCANS = 256
CHANNELS = 512
POSITIONS = 8192
OWNED = 512
LCMS_PARTS = 8
HALF = 256
BATCHES = (5, 1, 2, 2, 2, 2, 2, 3, 3, 8)
ORDER = (2, 6, 8, 9, 3, 7, 10, 14, 4, 11, 15, 5, 12, 13, 1)
WAITS = (2, 2, 2, 1, 1)
STEPS = (0, 0, 0, 4, 4)
FIT_FIRST = 7


def split(value):
    high = value.astype(BF16)
    low = (value - high.astype(F32)).astype(BF16)
    return high, low


def dot(left, right, dims, precision=None):
    return lax.dot_general(left, right, dims, precision=precision, preferred_element_type=F32)


def tree(terms):
    while len(terms) > 1:
        terms = [terms[i] + terms[i + 1] if i + 1 < len(terms) else terms[i] for i in range(0, len(terms), 2)]
    return terms[0]


def small_inverse(block):
    if len(block) == 2:
        scale = 1.0 / (block[0][0] * block[1][1] - block[0][1] * block[0][1])
        off = -block[0][1] * scale
        return [[block[1][1] * scale, off], [off, block[0][0] * scale]]
    size = len(block) // 2
    half = range(size)
    upper = small_inverse([[block[i][j] for j in half] for i in half])
    cross = [[block[i][size + j] for j in half] for i in half]
    mixed = [[tree([upper[i][k] * cross[k][j] for k in half]) for j in half] for i in half]
    rest = [[None] * size for _ in half]
    for i in half:
        for j in range(i, size):
            rest[i][j] = block[size + i][size + j] - tree([cross[k][i] * mixed[k][j] for k in half])
            rest[j][i] = rest[i][j]
    lower = small_inverse(rest)
    side = [[tree([mixed[i][k] * lower[k][j] for k in half]) for j in half] for i in half]
    result = [[None] * (2 * size) for _ in range(2 * size)]
    for i in half:
        for j in half:
            if j >= i:
                result[i][j] = upper[i][j] + tree([side[i][k] * mixed[j][k] for k in half])
                result[j][i] = result[i][j]
            result[i][size + j] = -side[i][j]
            result[size + j][i] = -side[i][j]
            result[size + i][size + j] = lower[i][j]
    return result


def elimination(matrix, found, pivot=8):
    size, wide = RANK, 2 * RANK
    lane = lax.broadcasted_iota(jnp.int32, (8, wide), 1)
    sub = lax.broadcasted_iota(jnp.int32, (8, wide), 0)
    tiles = []
    for t in range(size // 8):
        unit = (lane == sub + (size + 8 * t)).astype(F32)
        left = jnp.concatenate([matrix[8 * t : 8 * t + 8], jnp.zeros((8, size), F32)], axis=1)
        tiles.append(left + unit)
    for j in range(0, size, pivot):
        home, first = j // 8, j % 8
        rows = [jnp.broadcast_to(tiles[home][first + k : first + k + 1], (8, wide)) for k in range(pivot)]
        block = [[None] * pivot for _ in range(pivot)]
        for k in range(pivot):
            for m in range(k, pivot):
                block[k][m] = jnp.broadcast_to(rows[k][:, j + m : j + m + 1], (8, wide))
                block[m][k] = block[k][m]
        inverse = small_inverse(block)
        fresh = [tree([inverse[k][m] * rows[m] for m in range(pivot)]) for k in range(pivot)]
        for t in range(size // 8):
            tile = tiles[t]
            tile = tile - tree(
                [jnp.broadcast_to(tile[:, j + k : j + k + 1], (8, wide)) * fresh[k] for k in range(pivot)]
            )
            if t == home:
                for k in range(pivot):
                    tile = jnp.where(sub == first + k, fresh[k], tile)
            tiles[t] = tile
        yield
    found.append(jnp.concatenate([tile[:, size:] for tile in tiles], axis=0))


def spd_inverse(matrix):
    found = []
    for _ in elimination(matrix, found):
        pass
    return found[0]


def pack(value):
    return jnp.concatenate([value[0:32], value[32:64]], axis=1)


def unpack(value):
    return jnp.concatenate([value[:, 0:64], value[:, 64:128]], axis=0)


def twice(value):
    empty = jnp.zeros_like(value)
    return jnp.concatenate(
        [jnp.concatenate([value, empty], axis=1), jnp.concatenate([empty, value], axis=1)], axis=0
    )


def fold(value):
    wide = value[0:64] + value[64:128]
    return wide[:, 0:64] + wide[:, 64:128]


def kernel(
    lcms_hbm, spectra_hbm, scan_hbm, mz_hbm, ppm_hbm,
    sample_ref, new_ref,
    lcms_v, spectra_v, scan_v, mz_v, ppm_v, lcms_acc, columns_v,
    gram_out, gram_in, gram_all, right_in, right_all, fit_out, fit_in, ng_out, ng_in, ng_mz, ng_all, last_in,
    own_sem, lcms_sem, all_send, all_recv,
    gram_send, gram_recv, right_send, right_recv, share_send, share_recv,
    fit_send, fit_recv, ng_send, ng_recv, last_send, last_recv, lg_send, lg_recv, back_send, back_recv, whole_send, whole_recv, pair_sem,
):
    run = lax.axis_index("run")
    mz = lax.axis_index("mz")

    def run_peer(k):
        across = lax.rem(run // 8 + k // 8, 2)
        along = lax.rem(lax.rem(run // 2, 4) + (k // 2) % 4, 4)
        core = lax.rem(run + k % 2, 2)
        return ((across * 4 + along) * 2 + core, mz)

    def mz_peer(k):
        return (run, lax.rem(mz + k, N_MZ))

    loads = [
        pltpu.make_async_copy(mz_hbm, mz_v, own_sem.at[0]),
        pltpu.make_async_copy(scan_hbm, scan_v, own_sem.at[1]),
        pltpu.make_async_copy(ppm_hbm, ppm_v, own_sem.at[2]),
        pltpu.make_async_copy(spectra_hbm, spectra_v, own_sem.at[3]),
    ]
    for load in loads:
        load.start()
    per_part = RUNS // LCMS_PARTS // 2
    lcms_loads = [
        pltpu.make_async_copy(
            lcms_hbm.at[:, pl.ds(c * per_part, per_part)], lcms_v.at[:, pl.ds(c * per_part, per_part)], lcms_sem.at[c]
        )
        for c in range(LCMS_PARTS)
    ]
    begun = []

    def fetch(count):
        for load in lcms_loads[len(begun) : len(begun) + count]:
            load.start()
            begun.append(load)

    barrier = pltpu.get_barrier_semaphore()
    for k in range(1, N_RUN):
        pl.semaphore_signal(barrier, inc=1, device_id=run_peer(k), device_id_type=MESH)
    for k in range(1, N_MZ):
        pl.semaphore_signal(barrier, inc=1, device_id=mz_peer(k), device_id_type=MESH)
    pl.semaphore_wait(barrier, N_RUN + N_MZ - 2)

    def place(half):
        return columns_v.at[half, run // 4, :, pl.ds(pl.multiple_of(lax.rem(run, 4) * 32, 32), 32), :]

    def piece(owner, half):
        start = pl.multiple_of(owner * OWNED + half * HALF, HALF)
        return spectra_hbm.at[:, :, pl.ds(start, HALF)]

    fetch(1)
    own_pieces = [pltpu.make_async_copy(piece(run, h), place(h), own_sem.at[4 + h]) for h in range(2)]
    for copy in own_pieces:
        copy.start()
    spread = [[], []]
    for h in range(2):
        for k in ORDER:
            peer = run_peer(k)
            spread[h].append(pltpu.make_async_remote_copy(
                src_ref=piece(peer[0], h), dst_ref=place(h),
                send_sem=all_send.at[h, k], recv_sem=all_recv.at[h, k], device_id=peer, device_id_type=MESH,
            ))
    waiting = spread[0] + spread[1]

    batches = list(BATCHES)
    released = []

    def release():
        for copy in waiting[len(released) : len(released) + batches.pop(0)]:
            copy.start()
            released.append(copy)

    release()

    def exchange(peer_of, count, source_of, target, send, recv):
        copies = []
        for k in range(1, count):
            peer = peer_of(k)
            copies.append(pltpu.make_async_remote_copy(
                src_ref=source_of(peer), dst_ref=target,
                send_sem=send.at[k], recv_sem=recv.at[k], device_id=peer, device_id_type=MESH,
            ))
        for copy in copies:
            copy.start()
        return copies

    def arrive(copies):
        for copy in copies:
            copy.wait_recv()

    def total(ref, count):
        value = ref[0]
        for k in range(1, count):
            value = value + ref[k]
        return value

    for load in loads:
        load.wait()
    fetch(2)
    mz_high, mz_low = split(mz_v[...])
    mz_parts = jnp.concatenate([mz_high, mz_low], axis=0)
    mz_gram = fold(dot(mz_parts, mz_parts, NT))
    step = 1024
    sums = jnp.zeros((256, 128), F32)
    for c in range(POSITIONS // step):
        if c % 3 == 2:
            fetch(1)
        spec = jnp.concatenate([spectra_v[0, :, c * step : (c + 1) * step], spectra_v[1, :, c * step : (c + 1) * step]], axis=0)
        spec_high, spec_low = split(spec)
        ppm_high, ppm_low = split(ppm_v[:, c * step : (c + 1) * step])
        sums = sums + dot(
            jnp.concatenate([spec_high, spec_low, ppm_high, ppm_low], axis=0),
            jnp.concatenate([ppm_high, ppm_low], axis=0), NT,
        )
    nmr_local = fold(sums[0:128])
    ppm_gram = fold(sums[128:256])
    gram_out[...] = jnp.concatenate([mz_gram, ppm_gram], axis=1).reshape(N_MZ, 8, 128)
    gram_in[mz] = gram_out[mz]
    gram_copies = exchange(mz_peer, N_MZ, lambda peer: gram_out.at[peer[1]], gram_in.at[mz], gram_send, gram_recv)
    release()

    scan = scan_v[...]
    scan_gram = dot(scan, scan, NT, HIGHEST)
    scan_bf = scan.astype(BF16).astype(F32)
    scan_rows = jnp.concatenate([scan_bf, scan_bf], axis=0).T
    inverse_found = []
    part = 0
    for c, parts in enumerate(WAITS):
        for load in lcms_loads[part : part + parts]:
            load.wait()
        fetch(2)
        release()
        if c == 1:
            arrive(gram_copies)
            gram_all[mz] = total(gram_in, N_MZ)
            whole_copies = exchange(mz_peer, N_MZ, lambda peer: gram_all.at[mz], gram_all.at[mz], whole_send, whole_recv)
        if c == 3:
            arrive(whole_copies)
            grams = gram_all[...].reshape(64, 128)
            lcms_gram = scan_gram * grams[:, 0:64]
            steps = elimination(lcms_gram + grams[:, 64:128], inverse_found)
        for i in range(part * per_part, (part + parts) * per_part):
            for half in range(2):
                inner = dot(lcms_v[half, i], mz_parts, NT)
                lcms_acc[half, i : i + 1, :] = jnp.sum(inner * scan_rows, axis=0, keepdims=True)
        for _ in range(STEPS[c]):
            next(steps)
        part += parts
    for _ in steps:
        pass
    first_inverse = twice(inverse_found[0])
    lcms_packed = jnp.concatenate([lcms_acc[h, :, 0:64] + lcms_acc[h, :, 64:128] for h in range(2)], axis=1)
    right_in[mz] = lcms_packed + pack(nmr_local)
    right_copies = exchange(mz_peer, N_MZ, lambda peer: right_in.at[mz], right_in.at[mz], right_send, right_recv)
    release()

    arrive(right_copies)
    chip, core = run // 2, lax.rem(run, 2)
    right_all[chip, core] = total(right_in, N_MZ)
    mine = right_all.at[chip, core]
    share_copies = exchange(lambda k: run_peer(2 * k), N_RUN // 2, lambda peer: mine, mine, share_send, share_recv)
    release()
    arrive(share_copies)
    pair_copy = pltpu.make_async_remote_copy(
        src_ref=right_all.at[:, core], dst_ref=right_all.at[:, core],
        send_sem=pair_sem.at[0], recv_sem=pair_sem.at[1], device_id=run_peer(1), device_id_type=MESH,
    )
    pair_copy.start()
    release()
    arrive([pair_copy])
    first = dot(right_all[...].reshape(512, 128), first_inverse, NN, HIGHEST)
    products = dot(first, first, TN, HIGHEST)
    sample_gram = products[0:64, 0:64] + products[64:128, 64:128]
    weights = dot(first, twice(spd_inverse(sample_gram)), NN, HIGHEST).T

    rows = [slice(128 * g, 128 * g + 128) for g in range(4)]
    blocks = [block for g in range(4) for block in (weights[0:64, rows[g]], weights[64:128, rows[g]])]
    part_high, part_low = split(jnp.concatenate(blocks, axis=1))
    part_both = jnp.concatenate([part_high, part_low], axis=0)
    new_gram = jnp.zeros((RANK, RANK), F32)
    fits = []
    for h in range(2):
        own_pieces[h].wait()
        arrive(spread[h])
        high, low = split(columns_v[h].reshape(1024, HALF))
        both = dot(part_both, high, NN)
        ppm_new = (both[0:64] + both[64:128]) + dot(part_high, low, NN)
        new_ref[:, h * HALF : (h + 1) * HALF] = ppm_new
        new_high, new_low = split(ppm_new)
        new_parts = jnp.concatenate([new_high, new_low], axis=0)
        new_gram = new_gram + fold(dot(new_parts, new_parts, NT))
        if h == 1:
            packed = pack(new_gram)
            for k in range(N_RUN):
                ng_out[k] = packed[2 * k : 2 * k + 2]
            ng_in[run] = ng_out[run]
            ng_copies = exchange(run_peer, N_RUN, lambda peer: ng_out.at[peer[0]], ng_in.at[run], ng_send, ng_recv)
        both = dot(high, new_parts, NT) + dot(low, new_parts, NT)
        for g in range(4):
            fit = both[256 * g : 256 * g + 256, 0:64] + both[256 * g : 256 * g + 256, 64:128]
            fit = jnp.concatenate([fit[0:128], fit[128:256]], axis=1)
            if h == 0:
                fits.append(fit)
            else:
                fit_out[pl.ds(4 * g, 4)] = (fits[g] + fit).reshape(4, 32, 128)
    fit_in[run] = fit_out[run]

    def fit_batch(ks):
        copies = []
        for k in ks:
            peer = run_peer(k)
            copies.append(pltpu.make_async_remote_copy(
                src_ref=fit_out.at[peer[0]], dst_ref=fit_in.at[run],
                send_sem=fit_send.at[k], recv_sem=fit_recv.at[k], device_id=peer, device_id_type=MESH,
            ))
        for copy in copies:
            copy.start()
        return copies

    fit_copies = fit_batch(ORDER[:FIT_FIRST])
    arrive(ng_copies)
    ng_mz[mz] = total(ng_in, N_RUN)
    lg_copies = exchange(mz_peer, N_MZ, lambda peer: ng_mz.at[mz], ng_mz.at[mz], lg_send, lg_recv)
    fit_copies = fit_copies + fit_batch(ORDER[FIT_FIRST:])
    arrive(lg_copies)
    ng_all[run] = total(ng_mz, N_MZ)
    back_copies = exchange(run_peer, N_RUN, lambda peer: ng_all.at[run], ng_all.at[run], back_send, back_recv)
    arrive(fit_copies)
    last_in[mz] = total(fit_in, N_RUN) + lcms_packed
    last_copies = exchange(mz_peer, N_MZ, lambda peer: last_in.at[mz], last_in.at[mz], last_send, last_recv)
    arrive(back_copies)
    new_total = unpack(jnp.concatenate([ng_all[k] for k in range(N_RUN)], axis=0))
    last_inverse = twice(spd_inverse(lcms_gram + new_total))
    arrive(last_copies)
    sample_ref[...] = unpack(dot(total(last_in, N_MZ), last_inverse, NN, HIGHEST))

    for copies in (gram_copies, whole_copies, right_copies, share_copies, [pair_copy], ng_copies, fit_copies, lg_copies, back_copies, last_copies, waiting):
        for copy in copies:
            copy.wait_send()


def per_device(lcms, spectra, scan_factor, mz_factor, ppm_factor):
    hbm = pl.BlockSpec(memory_space=pltpu.HBM)
    vmem = pl.BlockSpec(memory_space=pltpu.VMEM)
    sems = pltpu.SemaphoreType.DMA
    return pl.pallas_call(
        kernel,
        out_shape=(
            jax.ShapeDtypeStruct((RUNS, RANK), F32),
            jax.ShapeDtypeStruct((RANK, OWNED), F32),
        ),
        in_specs=[hbm] * 5,
        out_specs=(vmem, vmem),
        scratch_shapes=[
            pltpu.VMEM((2, 32, SCANS, CHANNELS), BF16),
            pltpu.VMEM((2, 32, POSITIONS), F32),
            pltpu.VMEM((RANK, SCANS), F32),
            pltpu.VMEM((RANK, CHANNELS), F32),
            pltpu.VMEM((RANK, POSITIONS), F32),
            pltpu.VMEM((2, 32, 128), F32),
            pltpu.VMEM((2, 4, 2, 128, HALF), F32),
            pltpu.VMEM((N_MZ, 8, 128), F32),
            pltpu.VMEM((N_MZ, 8, 128), F32),
            pltpu.VMEM((N_MZ, 8, 128), F32),
            pltpu.VMEM((N_MZ, 32, 128), F32),
            pltpu.VMEM((N_RUN // 2, 2, 32, 128), F32),
            pltpu.VMEM((N_RUN, 32, 128), F32),
            pltpu.VMEM((N_RUN, 32, 128), F32),
            pltpu.VMEM((N_RUN, 2, 128), F32),
            pltpu.VMEM((N_RUN, 2, 128), F32),
            pltpu.VMEM((N_MZ, 2, 128), F32),
            pltpu.VMEM((N_RUN, 2, 128), F32),
            pltpu.VMEM((N_MZ, 32, 128), F32),
            sems((6,)), sems((LCMS_PARTS,)), sems((2, N_RUN)), sems((2, N_RUN)),
            sems((N_MZ,)), sems((N_MZ,)), sems((N_MZ,)), sems((N_MZ,)), sems((N_RUN,)), sems((N_RUN,)),
            sems((N_RUN,)), sems((N_RUN,)), sems((N_RUN,)), sems((N_RUN,)),
            sems((N_MZ,)), sems((N_MZ,)), sems((N_MZ,)), sems((N_MZ,)), sems((N_RUN,)), sems((N_RUN,)),
            sems((N_MZ,)), sems((N_MZ,)), sems((2,)),
        ],
        compiler_params=pltpu.CompilerParams(
            collective_id=0, has_side_effects=True, vmem_limit_bytes=60 * 2**20
        ),
    )(lcms.reshape(2, 32, SCANS, CHANNELS), spectra.reshape(2, 32, POSITIONS), scan_factor, mz_factor, ppm_factor)


def solution(mesh):
    return jax.shard_map(
        per_device,
        mesh=mesh,
        in_specs=(P("run", None, "mz"), P("run", "mz"), P(), P(None, "mz"), P(None, "mz")),
        out_specs=(P("run", None), P(None, ("mz", "run"))),
        check_vma=False,
    )
```

```python
import functools

import jax
import jax.numpy as jnp
from jax import lax
from jax.experimental import pallas as pl
from jax.experimental.pallas import tpu as pltpu
from jax.sharding import PartitionSpec as P

MESH = pl.DeviceIdType.MESH
HIGHEST = lax.Precision.HIGHEST
F32 = jnp.float32
BF16 = jnp.bfloat16
NT = (((1,), (1,)), ((), ()))
TN = (((0,), (0,)), ((), ()))
NN = (((1,), (0,)), ((), ()))

N_RUN = 16
N_MZ = 8
RANK = 64
RUNS = 64
SCANS = 256
CHANNELS = 512
POSITIONS = 8192
OWNED = 512
LCMS_PARTS = 8
HALF = 256
BATCHES = (5, 1, 2, 2, 2, 2, 2, 3, 3, 8)
ORDER = (2, 6, 8, 9, 3, 7, 10, 14, 4, 11, 15, 5, 12, 13, 1)
WAITS = (2, 2, 2, 1, 1)
STEPS = (0, 0, 0, 4, 4)


def split(value):
    high = value.astype(BF16)
    low = (value - high.astype(F32)).astype(BF16)
    return high, low


def dot(left, right, dims, precision=None):
    return lax.dot_general(left, right, dims, precision=precision, preferred_element_type=F32)


def tree(terms):
    while len(terms) > 1:
        terms = [terms[i] + terms[i + 1] if i + 1 < len(terms) else terms[i] for i in range(0, len(terms), 2)]
    return terms[0]


def small_inverse(block):
    if len(block) == 2:
        scale = 1.0 / (block[0][0] * block[1][1] - block[0][1] * block[0][1])
        off = -block[0][1] * scale
        return [[block[1][1] * scale, off], [off, block[0][0] * scale]]
    size = len(block) // 2
    half = range(size)
    upper = small_inverse([[block[i][j] for j in half] for i in half])
    cross = [[block[i][size + j] for j in half] for i in half]
    mixed = [[tree([upper[i][k] * cross[k][j] for k in half]) for j in half] for i in half]
    rest = [[None] * size for _ in half]
    for i in half:
        for j in range(i, size):
            rest[i][j] = block[size + i][size + j] - tree([cross[k][i] * mixed[k][j] for k in half])
            rest[j][i] = rest[i][j]
    lower = small_inverse(rest)
    side = [[tree([mixed[i][k] * lower[k][j] for k in half]) for j in half] for i in half]
    result = [[None] * (2 * size) for _ in range(2 * size)]
    for i in half:
        for j in half:
            if j >= i:
                result[i][j] = upper[i][j] + tree([side[i][k] * mixed[j][k] for k in half])
                result[j][i] = result[i][j]
            result[i][size + j] = -side[i][j]
            result[size + j][i] = -side[i][j]
            result[size + i][size + j] = lower[i][j]
    return result


def elimination(matrix, found, pivot=8):
    size, wide = RANK, 2 * RANK
    lane = lax.broadcasted_iota(jnp.int32, (8, wide), 1)
    sub = lax.broadcasted_iota(jnp.int32, (8, wide), 0)
    tiles = []
    for t in range(size // 8):
        unit = (lane == sub + (size + 8 * t)).astype(F32)
        left = jnp.concatenate([matrix[8 * t : 8 * t + 8], jnp.zeros((8, size), F32)], axis=1)
        tiles.append(left + unit)
    for j in range(0, size, pivot):
        home, first = j // 8, j % 8
        rows = [jnp.broadcast_to(tiles[home][first + k : first + k + 1], (8, wide)) for k in range(pivot)]
        block = [[None] * pivot for _ in range(pivot)]
        for k in range(pivot):
            for m in range(k, pivot):
                block[k][m] = jnp.broadcast_to(rows[k][:, j + m : j + m + 1], (8, wide))
                block[m][k] = block[k][m]
        inverse = small_inverse(block)
        fresh = [tree([inverse[k][m] * rows[m] for m in range(pivot)]) for k in range(pivot)]
        for t in range(size // 8):
            tile = tiles[t]
            tile = tile - tree(
                [jnp.broadcast_to(tile[:, j + k : j + k + 1], (8, wide)) * fresh[k] for k in range(pivot)]
            )
            if t == home:
                for k in range(pivot):
                    tile = jnp.where(sub == first + k, fresh[k], tile)
            tiles[t] = tile
        yield
    found.append(jnp.concatenate([tile[:, size:] for tile in tiles], axis=0))


def spd_inverse(matrix):
    found = []
    for _ in elimination(matrix, found):
        pass
    return found[0]


def pack(value):
    return jnp.concatenate([value[0:32], value[32:64]], axis=1)


def unpack(value):
    return jnp.concatenate([value[:, 0:64], value[:, 64:128]], axis=0)


def twice(value):
    empty = jnp.zeros_like(value)
    return jnp.concatenate(
        [jnp.concatenate([value, empty], axis=1), jnp.concatenate([empty, value], axis=1)], axis=0
    )


def fold(value):
    wide = value[0:64] + value[64:128]
    return wide[:, 0:64] + wide[:, 64:128]


def kernel(
    lcms_hbm, spectra_hbm, scan_hbm, mz_hbm, ppm_hbm,
    sample_ref, new_ref,
    lcms_v, spectra_v, scan_v, mz_v, ppm_v, lcms_acc, columns_v,
    gram_out, gram_in, gram_all, right_in, right_all, fit_out, pair_in, fit_mine, fit_in, ng_out, ng_in, ng_mz, ng_all, last_in,
    own_sem, lcms_sem, all_send, all_recv,
    gram_send, gram_recv, right_send, right_recv, share_send, share_recv,
    fit_send, fit_recv, ng_send, ng_recv, last_send, last_recv, lg_send, lg_recv, back_send, back_recv, whole_send, whole_recv, pair_sem,
):
    run = lax.axis_index("run")
    mz = lax.axis_index("mz")

    def run_peer(k):
        across = lax.rem(run // 8 + k // 8, 2)
        along = lax.rem(lax.rem(run // 2, 4) + (k // 2) % 4, 4)
        core = lax.rem(run + k % 2, 2)
        return ((across * 4 + along) * 2 + core, mz)

    def mz_peer(k):
        return (run, lax.rem(mz + k, N_MZ))

    loads = [
        pltpu.make_async_copy(mz_hbm, mz_v, own_sem.at[0]),
        pltpu.make_async_copy(scan_hbm, scan_v, own_sem.at[1]),
        pltpu.make_async_copy(ppm_hbm, ppm_v, own_sem.at[2]),
        pltpu.make_async_copy(spectra_hbm, spectra_v, own_sem.at[3]),
    ]
    for load in loads:
        load.start()
    per_part = RUNS // LCMS_PARTS // 2
    lcms_loads = [
        pltpu.make_async_copy(
            lcms_hbm.at[:, pl.ds(c * per_part, per_part)], lcms_v.at[:, pl.ds(c * per_part, per_part)], lcms_sem.at[c]
        )
        for c in range(LCMS_PARTS)
    ]
    begun = []

    def fetch(count):
        for load in lcms_loads[len(begun) : len(begun) + count]:
            load.start()
            begun.append(load)

    barrier = pltpu.get_barrier_semaphore()
    for k in range(1, N_RUN):
        pl.semaphore_signal(barrier, inc=1, device_id=run_peer(k), device_id_type=MESH)
    for k in range(1, N_MZ):
        pl.semaphore_signal(barrier, inc=1, device_id=mz_peer(k), device_id_type=MESH)
    pl.semaphore_wait(barrier, N_RUN + N_MZ - 2)

    def place(half):
        return columns_v.at[half, run // 4, :, pl.ds(pl.multiple_of(lax.rem(run, 4) * 32, 32), 32), :]

    def piece(owner, half):
        start = pl.multiple_of(owner * OWNED + half * HALF, HALF)
        return spectra_hbm.at[:, :, pl.ds(start, HALF)]

    fetch(1)
    own_pieces = [pltpu.make_async_copy(piece(run, h), place(h), own_sem.at[4 + h]) for h in range(2)]
    for copy in own_pieces:
        copy.start()
    spread = [[], []]
    for h in range(2):
        for k in ORDER:
            peer = run_peer(k)
            spread[h].append(pltpu.make_async_remote_copy(
                src_ref=piece(peer[0], h), dst_ref=place(h),
                send_sem=all_send.at[h, k], recv_sem=all_recv.at[h, k], device_id=peer, device_id_type=MESH,
            ))
    waiting = spread[0] + spread[1]

    batches = list(BATCHES)
    released = []

    def release():
        for copy in waiting[len(released) : len(released) + batches.pop(0)]:
            copy.start()
            released.append(copy)

    release()

    def exchange(peer_of, count, source_of, target, send, recv):
        copies = []
        for k in range(1, count):
            peer = peer_of(k)
            copies.append(pltpu.make_async_remote_copy(
                src_ref=source_of(peer), dst_ref=target,
                send_sem=send.at[k], recv_sem=recv.at[k], device_id=peer, device_id_type=MESH,
            ))
        for copy in copies:
            copy.start()
        return copies

    def arrive(copies):
        for copy in copies:
            copy.wait_recv()

    def total(ref, count):
        value = ref[0]
        for k in range(1, count):
            value = value + ref[k]
        return value

    for load in loads:
        load.wait()
    fetch(2)
    mz_high, mz_low = split(mz_v[...])
    mz_parts = jnp.concatenate([mz_high, mz_low], axis=0)
    mz_gram = fold(dot(mz_parts, mz_parts, NT))
    step = 1024
    sums = jnp.zeros((256, 128), F32)
    for c in range(POSITIONS // step):
        if c % 3 == 2:
            fetch(1)
        spec = jnp.concatenate([spectra_v[0, :, c * step : (c + 1) * step], spectra_v[1, :, c * step : (c + 1) * step]], axis=0)
        spec_high, spec_low = split(spec)
        ppm_high, ppm_low = split(ppm_v[:, c * step : (c + 1) * step])
        sums = sums + dot(
            jnp.concatenate([spec_high, spec_low, ppm_high, ppm_low], axis=0),
            jnp.concatenate([ppm_high, ppm_low], axis=0), NT,
        )
    nmr_local = fold(sums[0:128])
    ppm_gram = fold(sums[128:256])
    gram_out[...] = jnp.concatenate([mz_gram, ppm_gram], axis=1).reshape(N_MZ, 8, 128)
    gram_in[mz] = gram_out[mz]
    gram_copies = exchange(mz_peer, N_MZ, lambda peer: gram_out.at[peer[1]], gram_in.at[mz], gram_send, gram_recv)
    release()

    scan = scan_v[...]
    scan_gram = dot(scan, scan, NT, HIGHEST)
    scan_bf = scan.astype(BF16).astype(F32)
    scan_rows = jnp.concatenate([scan_bf, scan_bf], axis=0).T
    inverse_found = []
    part = 0
    for c, parts in enumerate(WAITS):
        for load in lcms_loads[part : part + parts]:
            load.wait()
        fetch(2)
        release()
        if c == 1:
            arrive(gram_copies)
            gram_all[mz] = total(gram_in, N_MZ)
            whole_copies = exchange(mz_peer, N_MZ, lambda peer: gram_all.at[mz], gram_all.at[mz], whole_send, whole_recv)
        if c == 3:
            arrive(whole_copies)
            grams = gram_all[...].reshape(64, 128)
            lcms_gram = scan_gram * grams[:, 0:64]
            steps = elimination(lcms_gram + grams[:, 64:128], inverse_found)
        for i in range(part * per_part, (part + parts) * per_part):
            for half in range(2):
                inner = dot(lcms_v[half, i], mz_parts, NT)
                lcms_acc[half, i : i + 1, :] = jnp.sum(inner * scan_rows, axis=0, keepdims=True)
        for _ in range(STEPS[c]):
            next(steps)
        part += parts
    for _ in steps:
        pass
    first_inverse = twice(inverse_found[0])
    lcms_packed = jnp.concatenate([lcms_acc[h, :, 0:64] + lcms_acc[h, :, 64:128] for h in range(2)], axis=1)
    right_in[mz] = lcms_packed + pack(nmr_local)
    right_copies = exchange(mz_peer, N_MZ, lambda peer: right_in.at[mz], right_in.at[mz], right_send, right_recv)
    release()

    arrive(right_copies)
    chip, core = run // 2, lax.rem(run, 2)
    right_all[chip, core] = total(right_in, N_MZ)
    mine = right_all.at[chip, core]
    share_copies = exchange(lambda k: run_peer(2 * k), N_RUN // 2, lambda peer: mine, mine, share_send, share_recv)
    release()
    arrive(share_copies)
    pair_copy = pltpu.make_async_remote_copy(
        src_ref=right_all.at[:, core], dst_ref=right_all.at[:, core],
        send_sem=pair_sem.at[0], recv_sem=pair_sem.at[1], device_id=run_peer(1), device_id_type=MESH,
    )
    pair_copy.start()
    release()
    arrive([pair_copy])
    first = dot(right_all[...].reshape(512, 128), first_inverse, NN, HIGHEST)
    products = dot(first, first, TN, HIGHEST)
    sample_gram = products[0:64, 0:64] + products[64:128, 64:128]
    weights = dot(first, twice(spd_inverse(sample_gram)), NN, HIGHEST).T

    rows = [slice(128 * g, 128 * g + 128) for g in range(4)]
    blocks = [block for g in range(4) for block in (weights[0:64, rows[g]], weights[64:128, rows[g]])]
    part_high, part_low = split(jnp.concatenate(blocks, axis=1))
    part_both = jnp.concatenate([part_high, part_low], axis=0)
    new_gram = jnp.zeros((RANK, RANK), F32)
    fits = []
    for h in range(2):
        own_pieces[h].wait()
        arrive(spread[h])
        high, low = split(columns_v[h].reshape(1024, HALF))
        both = dot(part_both, high, NN)
        ppm_new = (both[0:64] + both[64:128]) + dot(part_high, low, NN)
        new_ref[:, h * HALF : (h + 1) * HALF] = ppm_new
        new_high, new_low = split(ppm_new)
        new_parts = jnp.concatenate([new_high, new_low], axis=0)
        new_gram = new_gram + fold(dot(new_parts, new_parts, NT))
        if h == 1:
            packed = pack(new_gram)
            for k in range(N_RUN):
                ng_out[k] = packed[2 * k : 2 * k + 2]
            ng_in[run] = ng_out[run]
            ng_copies = exchange(run_peer, N_RUN, lambda peer: ng_out.at[peer[0]], ng_in.at[run], ng_send, ng_recv)
        both = dot(high, new_parts, NT) + dot(low, new_parts, NT)
        for g in range(4):
            fit = both[256 * g : 256 * g + 256, 0:64] + both[256 * g : 256 * g + 256, 64:128]
            fit = jnp.concatenate([fit[0:128], fit[128:256]], axis=1)
            if h == 0:
                fits.append(fit)
            else:
                fit_out[pl.ds(2 * g, 2)] = (fits[g] + fit).reshape(2, 2, 32, 128)
    fit_pair = pltpu.make_async_remote_copy(
        src_ref=fit_out.at[:, 1 - core], dst_ref=pair_in,
        send_sem=pair_sem.at[2], recv_sem=pair_sem.at[3], device_id=run_peer(1), device_id_type=MESH,
    )
    fit_pair.start()
    arrive([fit_pair])
    fit_mine[...] = fit_out[:, core] + pair_in[...]
    fit_in[chip] = fit_mine[chip]
    fit_copies = exchange(
        lambda k: run_peer(2 * k), N_RUN // 2, lambda peer: fit_mine.at[peer[0] // 2], fit_in.at[chip], fit_send, fit_recv
    )
    arrive(ng_copies)
    ng_mz[mz] = total(ng_in, N_RUN)
    lg_copies = exchange(mz_peer, N_MZ, lambda peer: ng_mz.at[mz], ng_mz.at[mz], lg_send, lg_recv)
    arrive(lg_copies)
    ng_all[run] = total(ng_mz, N_MZ)
    back_copies = exchange(run_peer, N_RUN, lambda peer: ng_all.at[run], ng_all.at[run], back_send, back_recv)
    arrive(fit_copies)
    last_in[mz] = total(fit_in, N_RUN // 2) + lcms_packed
    last_copies = exchange(mz_peer, N_MZ, lambda peer: last_in.at[mz], last_in.at[mz], last_send, last_recv)
    arrive(back_copies)
    new_total = unpack(jnp.concatenate([ng_all[k] for k in range(N_RUN)], axis=0))
    last_inverse = twice(spd_inverse(lcms_gram + new_total))
    arrive(last_copies)
    sample_ref[...] = unpack(dot(total(last_in, N_MZ), last_inverse, NN, HIGHEST))

    for copies in (gram_copies, whole_copies, right_copies, share_copies, [pair_copy, fit_pair], ng_copies, fit_copies, lg_copies, back_copies, last_copies, waiting):
        for copy in copies:
            copy.wait_send()


def deliver(sample_ref, new_ref, sample_out, new_out):
    sample_out[...] = sample_ref[...]
    new_out[...] = new_ref[...]


def per_device(lcms, spectra, scan_factor, mz_factor, ppm_factor):
    hbm = pl.BlockSpec(memory_space=pltpu.HBM)
    vmem = pl.BlockSpec(memory_space=pltpu.VMEM)
    sems = pltpu.SemaphoreType.DMA
    shapes = (
        jax.ShapeDtypeStruct((RUNS, RANK), F32),
        jax.ShapeDtypeStruct((RANK, OWNED), F32),
    )
    results = pl.pallas_call(
        kernel,
        out_shape=shapes,
        in_specs=[hbm] * 5,
        out_specs=(vmem, vmem),
        scratch_shapes=[
            pltpu.VMEM((2, 32, SCANS, CHANNELS), BF16),
            pltpu.VMEM((2, 32, POSITIONS), F32),
            pltpu.VMEM((RANK, SCANS), F32),
            pltpu.VMEM((RANK, CHANNELS), F32),
            pltpu.VMEM((RANK, POSITIONS), F32),
            pltpu.VMEM((2, 32, 128), F32),
            pltpu.VMEM((2, 4, 2, 128, HALF), F32),
            pltpu.VMEM((N_MZ, 8, 128), F32),
            pltpu.VMEM((N_MZ, 8, 128), F32),
            pltpu.VMEM((N_MZ, 8, 128), F32),
            pltpu.VMEM((N_MZ, 32, 128), F32),
            pltpu.VMEM((N_RUN // 2, 2, 32, 128), F32),
            pltpu.VMEM((N_RUN // 2, 2, 32, 128), F32),
            pltpu.VMEM((N_RUN // 2, 32, 128), F32),
            pltpu.VMEM((N_RUN // 2, 32, 128), F32),
            pltpu.VMEM((N_RUN // 2, 32, 128), F32),
            pltpu.VMEM((N_RUN, 2, 128), F32),
            pltpu.VMEM((N_RUN, 2, 128), F32),
            pltpu.VMEM((N_MZ, 2, 128), F32),
            pltpu.VMEM((N_RUN, 2, 128), F32),
            pltpu.VMEM((N_MZ, 32, 128), F32),
            sems((6,)), sems((LCMS_PARTS,)), sems((2, N_RUN)), sems((2, N_RUN)),
            sems((N_MZ,)), sems((N_MZ,)), sems((N_MZ,)), sems((N_MZ,)), sems((N_RUN,)), sems((N_RUN,)),
            sems((N_RUN,)), sems((N_RUN,)), sems((N_RUN,)), sems((N_RUN,)),
            sems((N_MZ,)), sems((N_MZ,)), sems((N_MZ,)), sems((N_MZ,)), sems((N_RUN,)), sems((N_RUN,)),
            sems((N_MZ,)), sems((N_MZ,)), sems((4,)),
        ],
        compiler_params=pltpu.CompilerParams(
            collective_id=0, has_side_effects=True, vmem_limit_bytes=60 * 2**20
        ),
    )(lcms.reshape(2, 32, SCANS, CHANNELS), spectra.reshape(2, 32, POSITIONS), scan_factor, mz_factor, ppm_factor)
    return pl.pallas_call(
        deliver,
        out_shape=shapes,
        in_specs=[vmem] * 2,
        out_specs=(vmem, vmem),
    )(*results)


def solution(mesh):
    return jax.shard_map(
        per_device,
        mesh=mesh,
        in_specs=(P("run", None, "mz"), P("run", "mz"), P(), P(None, "mz"), P(None, "mz")),
        out_specs=(P("run", None), P(None, ("mz", "run"))),
        check_vma=False,
    )
```

```python
import functools

import jax
import jax.numpy as jnp
from jax import lax
from jax.experimental import pallas as pl
from jax.experimental.pallas import tpu as pltpu
from jax.sharding import PartitionSpec as P

MESH = pl.DeviceIdType.MESH
HIGHEST = lax.Precision.HIGHEST
F32 = jnp.float32
BF16 = jnp.bfloat16
NT = (((1,), (1,)), ((), ()))
TN = (((0,), (0,)), ((), ()))
NN = (((1,), (0,)), ((), ()))

N_RUN = 16
N_MZ = 8
RANK = 64
RUNS = 64
SCANS = 256
CHANNELS = 512
POSITIONS = 8192
OWNED = 512
LCMS_PARTS = 8
HALF = 256
BATCHES = (5, 1, 2, 2, 2, 2, 2, 3, 3, 8)
ORDER = (2, 6, 8, 9, 3, 7, 10, 14, 4, 11, 15, 5, 12, 13, 1)
WAITS = (2, 2, 2, 1, 1)
STEPS = (0, 0, 0, 4, 4)


def split(value):
    high = value.astype(BF16)
    low = (value - high.astype(F32)).astype(BF16)
    return high, low


def dot(left, right, dims, precision=None):
    return lax.dot_general(left, right, dims, precision=precision, preferred_element_type=F32)


def tree(terms):
    while len(terms) > 1:
        terms = [terms[i] + terms[i + 1] if i + 1 < len(terms) else terms[i] for i in range(0, len(terms), 2)]
    return terms[0]


def small_inverse(block):
    if len(block) == 2:
        scale = 1.0 / (block[0][0] * block[1][1] - block[0][1] * block[0][1])
        off = -block[0][1] * scale
        return [[block[1][1] * scale, off], [off, block[0][0] * scale]]
    size = len(block) // 2
    half = range(size)
    upper = small_inverse([[block[i][j] for j in half] for i in half])
    cross = [[block[i][size + j] for j in half] for i in half]
    mixed = [[tree([upper[i][k] * cross[k][j] for k in half]) for j in half] for i in half]
    rest = [[None] * size for _ in half]
    for i in half:
        for j in range(i, size):
            rest[i][j] = block[size + i][size + j] - tree([cross[k][i] * mixed[k][j] for k in half])
            rest[j][i] = rest[i][j]
    lower = small_inverse(rest)
    side = [[tree([mixed[i][k] * lower[k][j] for k in half]) for j in half] for i in half]
    result = [[None] * (2 * size) for _ in range(2 * size)]
    for i in half:
        for j in half:
            if j >= i:
                result[i][j] = upper[i][j] + tree([side[i][k] * mixed[j][k] for k in half])
                result[j][i] = result[i][j]
            result[i][size + j] = -side[i][j]
            result[size + j][i] = -side[i][j]
            result[size + i][size + j] = lower[i][j]
    return result


def elimination(matrix, found, pivot=8):
    size, wide = RANK, 2 * RANK
    lane = lax.broadcasted_iota(jnp.int32, (8, wide), 1)
    sub = lax.broadcasted_iota(jnp.int32, (8, wide), 0)
    tiles = []
    for t in range(size // 8):
        unit = (lane == sub + (size + 8 * t)).astype(F32)
        left = jnp.concatenate([matrix[8 * t : 8 * t + 8], jnp.zeros((8, size), F32)], axis=1)
        tiles.append(left + unit)
    for j in range(0, size, pivot):
        home, first = j // 8, j % 8
        rows = [jnp.broadcast_to(tiles[home][first + k : first + k + 1], (8, wide)) for k in range(pivot)]
        block = [[None] * pivot for _ in range(pivot)]
        for k in range(pivot):
            for m in range(k, pivot):
                block[k][m] = jnp.broadcast_to(rows[k][:, j + m : j + m + 1], (8, wide))
                block[m][k] = block[k][m]
        inverse = small_inverse(block)
        fresh = [tree([inverse[k][m] * rows[m] for m in range(pivot)]) for k in range(pivot)]
        for t in range(size // 8):
            tile = tiles[t]
            tile = tile - tree(
                [jnp.broadcast_to(tile[:, j + k : j + k + 1], (8, wide)) * fresh[k] for k in range(pivot)]
            )
            if t == home:
                for k in range(pivot):
                    tile = jnp.where(sub == first + k, fresh[k], tile)
            tiles[t] = tile
        yield
    found.append(jnp.concatenate([tile[:, size:] for tile in tiles], axis=0))


def spd_inverse(matrix):
    found = []
    for _ in elimination(matrix, found):
        pass
    return found[0]


def pack(value):
    return jnp.concatenate([value[0:32], value[32:64]], axis=1)


def unpack(value):
    return jnp.concatenate([value[:, 0:64], value[:, 64:128]], axis=0)


def twice(value):
    empty = jnp.zeros_like(value)
    return jnp.concatenate(
        [jnp.concatenate([value, empty], axis=1), jnp.concatenate([empty, value], axis=1)], axis=0
    )


def fold(value):
    wide = value[0:64] + value[64:128]
    return wide[:, 0:64] + wide[:, 64:128]


def kernel(
    lcms_hbm, spectra_hbm, scan_hbm, mz_hbm, ppm_hbm,
    sample_ref, new_ref,
    lcms_v, spectra_v, scan_v, mz_v, ppm_v, lcms_acc, columns_v,
    gram_out, gram_in, gram_all, right_in, right_all, fit_out, pair_in, fit_mine, fit_in, ng_out, ng_in, ng_mz, ng_all, last_in,
    own_sem, lcms_sem, all_send, all_recv,
    gram_send, gram_recv, right_send, right_recv, share_send, share_recv,
    fit_send, fit_recv, ng_send, ng_recv, last_send, last_recv, lg_send, lg_recv, back_send, back_recv, whole_send, whole_recv, pair_sem,
):
    run = lax.axis_index("run")
    mz = lax.axis_index("mz")

    def run_peer(k):
        across = lax.rem(run // 8 + k // 8, 2)
        along = lax.rem(lax.rem(run // 2, 4) + (k // 2) % 4, 4)
        core = lax.rem(run + k % 2, 2)
        return ((across * 4 + along) * 2 + core, mz)

    def mz_peer(k):
        return (run, lax.rem(mz + k, N_MZ))

    loads = [
        pltpu.make_async_copy(mz_hbm, mz_v, own_sem.at[0]),
        pltpu.make_async_copy(scan_hbm, scan_v, own_sem.at[1]),
        pltpu.make_async_copy(ppm_hbm, ppm_v, own_sem.at[2]),
        pltpu.make_async_copy(spectra_hbm, spectra_v, own_sem.at[3]),
    ]
    for load in loads:
        load.start()
    per_part = RUNS // LCMS_PARTS // 2
    lcms_loads = [
        pltpu.make_async_copy(
            lcms_hbm.at[:, pl.ds(c * per_part, per_part)], lcms_v.at[:, pl.ds(c * per_part, per_part)], lcms_sem.at[c]
        )
        for c in range(LCMS_PARTS)
    ]
    begun = []

    def fetch(count):
        for load in lcms_loads[len(begun) : len(begun) + count]:
            load.start()
            begun.append(load)

    barrier = pltpu.get_barrier_semaphore()
    for k in range(1, N_RUN):
        pl.semaphore_signal(barrier, inc=1, device_id=run_peer(k), device_id_type=MESH)
    for k in range(1, N_MZ):
        pl.semaphore_signal(barrier, inc=1, device_id=mz_peer(k), device_id_type=MESH)
    pl.semaphore_wait(barrier, N_RUN + N_MZ - 2)

    def place(half):
        return columns_v.at[half, run // 4, :, pl.ds(pl.multiple_of(lax.rem(run, 4) * 32, 32), 32), :]

    def piece(owner, half):
        start = pl.multiple_of(owner * OWNED + half * HALF, HALF)
        return spectra_hbm.at[:, :, pl.ds(start, HALF)]

    fetch(1)
    own_pieces = [pltpu.make_async_copy(piece(run, h), place(h), own_sem.at[4 + h]) for h in range(2)]
    for copy in own_pieces:
        copy.start()
    spread = [[], []]
    for h in range(2):
        for k in ORDER:
            peer = run_peer(k)
            spread[h].append(pltpu.make_async_remote_copy(
                src_ref=piece(peer[0], h), dst_ref=place(h),
                send_sem=all_send.at[h, k], recv_sem=all_recv.at[h, k], device_id=peer, device_id_type=MESH,
            ))
    waiting = spread[0] + spread[1]

    batches = list(BATCHES)
    released = []

    def release():
        for copy in waiting[len(released) : len(released) + batches.pop(0)]:
            copy.start()
            released.append(copy)

    release()

    def exchange(peer_of, count, source_of, target, send, recv):
        copies = []
        for k in range(1, count):
            peer = peer_of(k)
            copies.append(pltpu.make_async_remote_copy(
                src_ref=source_of(peer), dst_ref=target,
                send_sem=send.at[k], recv_sem=recv.at[k], device_id=peer, device_id_type=MESH,
            ))
        for copy in copies:
            copy.start()
        return copies

    def arrive(copies):
        for copy in copies:
            copy.wait_recv()

    def total(ref, count):
        value = ref[0]
        for k in range(1, count):
            value = value + ref[k]
        return value

    for load in loads:
        load.wait()
    fetch(2)
    mz_high, mz_low = split(mz_v[...])
    mz_parts = jnp.concatenate([mz_high, mz_low], axis=0)
    mz_gram = fold(dot(mz_parts, mz_parts, NT))
    step = 1024
    sums = jnp.zeros((256, 128), F32)
    for c in range(POSITIONS // step):
        if c % 3 == 2:
            fetch(1)
        spec = jnp.concatenate([spectra_v[0, :, c * step : (c + 1) * step], spectra_v[1, :, c * step : (c + 1) * step]], axis=0)
        spec_high, spec_low = split(spec)
        ppm_high, ppm_low = split(ppm_v[:, c * step : (c + 1) * step])
        sums = sums + dot(
            jnp.concatenate([spec_high, spec_low, ppm_high, ppm_low], axis=0),
            jnp.concatenate([ppm_high, ppm_low], axis=0), NT,
        )
    nmr_local = fold(sums[0:128])
    ppm_gram = fold(sums[128:256])
    gram_out[...] = jnp.concatenate([mz_gram, ppm_gram], axis=1).reshape(N_MZ, 8, 128)
    gram_in[mz] = gram_out[mz]
    gram_copies = exchange(mz_peer, N_MZ, lambda peer: gram_out.at[peer[1]], gram_in.at[mz], gram_send, gram_recv)
    release()

    scan = scan_v[...]
    scan_gram = dot(scan, scan, NT, HIGHEST)
    scan_bf = scan.astype(BF16).astype(F32)
    scan_rows = jnp.concatenate([scan_bf, scan_bf], axis=0).T
    inverse_found = []
    part = 0
    for c, parts in enumerate(WAITS):
        for load in lcms_loads[part : part + parts]:
            load.wait()
        fetch(2)
        release()
        if c == 1:
            arrive(gram_copies)
            gram_all[mz] = total(gram_in, N_MZ)
            whole_copies = exchange(mz_peer, N_MZ, lambda peer: gram_all.at[mz], gram_all.at[mz], whole_send, whole_recv)
        if c == 3:
            arrive(whole_copies)
            grams = gram_all[...].reshape(64, 128)
            lcms_gram = scan_gram * grams[:, 0:64]
            steps = elimination(lcms_gram + grams[:, 64:128], inverse_found)
        for i in range(part * per_part, (part + parts) * per_part):
            for half in range(2):
                inner = dot(lcms_v[half, i], mz_parts, NT)
                lcms_acc[half, i : i + 1, :] = jnp.sum(inner * scan_rows, axis=0, keepdims=True)
        for _ in range(STEPS[c]):
            next(steps)
        part += parts
    for _ in steps:
        pass
    first_inverse = twice(inverse_found[0])
    lcms_packed = jnp.concatenate([lcms_acc[h, :, 0:64] + lcms_acc[h, :, 64:128] for h in range(2)], axis=1)
    right_in[mz] = lcms_packed + pack(nmr_local)
    right_copies = exchange(mz_peer, N_MZ, lambda peer: right_in.at[mz], right_in.at[mz], right_send, right_recv)
    release()

    arrive(right_copies)
    chip, core = run // 2, lax.rem(run, 2)
    right_all[chip, core] = total(right_in, N_MZ)
    mine = right_all.at[chip, core]
    share_copies = exchange(lambda k: run_peer(2 * k), N_RUN // 2, lambda peer: mine, mine, share_send, share_recv)
    release()
    arrive(share_copies)
    pair_copy = pltpu.make_async_remote_copy(
        src_ref=right_all.at[:, core], dst_ref=right_all.at[:, core],
        send_sem=pair_sem.at[0], recv_sem=pair_sem.at[1], device_id=run_peer(1), device_id_type=MESH,
    )
    pair_copy.start()
    release()
    arrive([pair_copy])
    first = dot(right_all[...].reshape(512, 128), first_inverse, NN, HIGHEST)
    products = dot(first, first, TN, HIGHEST)
    sample_gram = products[0:64, 0:64] + products[64:128, 64:128]
    weights = dot(first, twice(spd_inverse(sample_gram)), NN, HIGHEST).T

    rows = [slice(128 * g, 128 * g + 128) for g in range(4)]
    blocks = [block for g in range(4) for block in (weights[0:64, rows[g]], weights[64:128, rows[g]])]
    part_high, part_low = split(jnp.concatenate(blocks, axis=1))
    part_both = jnp.concatenate([part_high, part_low], axis=0)
    new_gram = jnp.zeros((RANK, RANK), F32)
    fits = []
    for h in range(2):
        own_pieces[h].wait()
        arrive(spread[h])
        high, low = split(columns_v[h].reshape(1024, HALF))
        both = dot(part_both, high, NN)
        ppm_new = (both[0:64] + both[64:128]) + dot(part_high, low, NN)
        new_ref[:, h * HALF : (h + 1) * HALF] = ppm_new
        new_high, new_low = split(ppm_new)
        new_parts = jnp.concatenate([new_high, new_low], axis=0)
        new_gram = new_gram + fold(dot(new_parts, new_parts, NT))
        if h == 1:
            packed = pack(new_gram)
            for k in range(N_RUN):
                ng_out[k] = packed[2 * k : 2 * k + 2]
            ng_in[run] = ng_out[run]
            ng_copies = exchange(run_peer, N_RUN, lambda peer: ng_out.at[peer[0]], ng_in.at[run], ng_send, ng_recv)
        both = dot(high, new_parts, NT) + dot(low, new_parts, NT)
        for g in range(4):
            fit = both[256 * g : 256 * g + 256, 0:64] + both[256 * g : 256 * g + 256, 64:128]
            fit = jnp.concatenate([fit[0:128], fit[128:256]], axis=1)
            if h == 0:
                fits.append(fit)
            else:
                fit_out[pl.ds(2 * g, 2)] = (fits[g] + fit).reshape(2, 2, 32, 128)
    fit_pair = pltpu.make_async_remote_copy(
        src_ref=fit_out.at[:, 1 - core], dst_ref=pair_in,
        send_sem=pair_sem.at[2], recv_sem=pair_sem.at[3], device_id=run_peer(1), device_id_type=MESH,
    )
    fit_pair.start()
    arrive(ng_copies)
    ng_mz[mz] = total(ng_in, N_RUN)
    lg_copies = exchange(mz_peer, N_MZ, lambda peer: ng_mz.at[mz], ng_mz.at[mz], lg_send, lg_recv)
    arrive([fit_pair])
    fit_mine[...] = fit_out[:, core] + pair_in[...]
    fit_in[chip] = fit_mine[chip]
    fit_copies = exchange(
        lambda k: run_peer(2 * k), N_RUN // 2, lambda peer: fit_mine.at[peer[0] // 2], fit_in.at[chip], fit_send, fit_recv
    )
    arrive(lg_copies)
    ng_all[run] = total(ng_mz, N_MZ)
    back_copies = exchange(run_peer, N_RUN, lambda peer: ng_all.at[run], ng_all.at[run], back_send, back_recv)
    arrive(fit_copies)
    last_in[mz] = total(fit_in, N_RUN // 2) + lcms_packed
    last_copies = exchange(mz_peer, N_MZ, lambda peer: last_in.at[mz], last_in.at[mz], last_send, last_recv)
    arrive(back_copies)
    new_total = unpack(jnp.concatenate([ng_all[k] for k in range(N_RUN)], axis=0))
    last_inverse = twice(spd_inverse(lcms_gram + new_total))
    arrive(last_copies)
    sample_ref[...] = unpack(dot(total(last_in, N_MZ), last_inverse, NN, HIGHEST))

    for copies in (gram_copies, whole_copies, right_copies, share_copies, [pair_copy, fit_pair], ng_copies, fit_copies, lg_copies, back_copies, last_copies, waiting):
        for copy in copies:
            copy.wait_send()


def deliver(sample_ref, new_ref, sample_out, new_out):
    sample_out[...] = sample_ref[...]
    new_out[...] = new_ref[...]


def per_device(lcms, spectra, scan_factor, mz_factor, ppm_factor):
    hbm = pl.BlockSpec(memory_space=pltpu.HBM)
    vmem = pl.BlockSpec(memory_space=pltpu.VMEM)
    sems = pltpu.SemaphoreType.DMA
    shapes = (
        jax.ShapeDtypeStruct((RUNS, RANK), F32),
        jax.ShapeDtypeStruct((RANK, OWNED), F32),
    )
    results = pl.pallas_call(
        kernel,
        out_shape=shapes,
        in_specs=[hbm] * 5,
        out_specs=(vmem, vmem),
        scratch_shapes=[
            pltpu.VMEM((2, 32, SCANS, CHANNELS), BF16),
            pltpu.VMEM((2, 32, POSITIONS), F32),
            pltpu.VMEM((RANK, SCANS), F32),
            pltpu.VMEM((RANK, CHANNELS), F32),
            pltpu.VMEM((RANK, POSITIONS), F32),
            pltpu.VMEM((2, 32, 128), F32),
            pltpu.VMEM((2, 4, 2, 128, HALF), F32),
            pltpu.VMEM((N_MZ, 8, 128), F32),
            pltpu.VMEM((N_MZ, 8, 128), F32),
            pltpu.VMEM((N_MZ, 8, 128), F32),
            pltpu.VMEM((N_MZ, 32, 128), F32),
            pltpu.VMEM((N_RUN // 2, 2, 32, 128), F32),
            pltpu.VMEM((N_RUN // 2, 2, 32, 128), F32),
            pltpu.VMEM((N_RUN // 2, 32, 128), F32),
            pltpu.VMEM((N_RUN // 2, 32, 128), F32),
            pltpu.VMEM((N_RUN // 2, 32, 128), F32),
            pltpu.VMEM((N_RUN, 2, 128), F32),
            pltpu.VMEM((N_RUN, 2, 128), F32),
            pltpu.VMEM((N_MZ, 2, 128), F32),
            pltpu.VMEM((N_RUN, 2, 128), F32),
            pltpu.VMEM((N_MZ, 32, 128), F32),
            sems((6,)), sems((LCMS_PARTS,)), sems((2, N_RUN)), sems((2, N_RUN)),
            sems((N_MZ,)), sems((N_MZ,)), sems((N_MZ,)), sems((N_MZ,)), sems((N_RUN,)), sems((N_RUN,)),
            sems((N_RUN,)), sems((N_RUN,)), sems((N_RUN,)), sems((N_RUN,)),
            sems((N_MZ,)), sems((N_MZ,)), sems((N_MZ,)), sems((N_MZ,)), sems((N_RUN,)), sems((N_RUN,)),
            sems((N_MZ,)), sems((N_MZ,)), sems((4,)),
        ],
        compiler_params=pltpu.CompilerParams(
            collective_id=0, has_side_effects=True, vmem_limit_bytes=60 * 2**20
        ),
    )(lcms.reshape(2, 32, SCANS, CHANNELS), spectra.reshape(2, 32, POSITIONS), scan_factor, mz_factor, ppm_factor)
    return pl.pallas_call(
        deliver,
        out_shape=shapes,
        in_specs=[vmem] * 2,
        out_specs=(vmem, vmem),
    )(*results)


def solution(mesh):
    return jax.shard_map(
        per_device,
        mesh=mesh,
        in_specs=(P("run", None, "mz"), P("run", "mz"), P(), P(None, "mz"), P(None, "mz")),
        out_specs=(P("run", None), P(None, ("mz", "run"))),
        check_vma=False,
    )
```
